32 devices in a mesh: band: 16 (over z, x, core), domain: 2 (over y).
Axes of the slice: x: 2, y: 2, z: 4, core: 2. Of those that a mesh axis runs over, the one named last changes fastest.
Arguments:
- orbitals: float32 [256, 16, 4096], P('band', 'domain'), may hold values from -6 to 6
- previous: float32 [256, 16, 4096], P('band', 'domain'), may hold values from -6 to 6
- potential: float32 [16, 4096], P('domain'), may hold values from -3 to 3
- rotation: float32 [256, 256], P(None, 'band'), may hold values from -1 to 1
- accumulated: float32 [256, 16, 4096], P('band', 'domain'), may hold values from -6 to 6
- panel: int32 [1], replicated, may hold values from 0 to 65535
Outputs:
- filtered: float32 [256, 16, 4096], P('band', 'domain')
- rotated: float32 [256, 16, 4096], P('band', 'domain')
The draws below stay inside these ranges and needn't reach their ends.
All inputs are finite; a program needn't handle non-finite values.
Results may differ from the reference program's by a relative error of at most 0.000059.
Values sent between devices are 32-bit elements; how exact they have to be, the bound alone decides.
A program may use at most 192 MiB of HBM per device.

```python
import jax
import jax.numpy as jnp
from jax import lax

ORB_DEV = 16
NY = 64
NX = 64
ORBS = 256
PANEL = 32
NZ = 16
N_BAND = 16


def block_scale(rng, shape, split, low, top_value):
    loudness = 1.0
    for dim, parts in split:
        heights = jax.random.uniform(jax.random.fold_in(jax.random.fold_in(rng, 6), dim), (parts,), jnp.float32, low / len(split), top_value / len(split))
        loudness = loudness * jnp.repeat(jnp.exp(heights), shape[dim] // parts).reshape((-1,) + (1,) * (len(shape) - 1 - dim))
    return loudness


def noise(stream_key, shape, width, limit, pieces=(), dtype=jnp.bfloat16):
    level = block_scale(stream_key, shape, pieces, -0.22, 0.18) if pieces else 1.0
    entries = jax.random.normal(stream_key, shape, jnp.float32) * width * level
    return jnp.minimum(jnp.maximum(entries, -limit), limit).astype(dtype)


def setup_inputs(seed: int = 0) -> dict:
    key_list = jax.random.split(jax.random.key(seed), 7)
    return {
        "orbitals": noise(key_list[0], (ORBS, NZ, NY * NX), 1.0, 6.0, ((0, 16), (1, 2)), jnp.float32),
        "previous": noise(key_list[1], (ORBS, NZ, NY * NX), 1.0, 6.0, ((0, 16), (1, 2)), jnp.float32),
        "potential": jnp.clip(jax.random.uniform(key_list[2], (NZ, NY * NX), jnp.float32, -3.0, 3.0) * block_scale(key_list[2], (NZ, NY * NX), ((0, 2),), -0.4, 0.0), -3.0, 3.0),
        "rotation": noise(key_list[3], (ORBS, ORBS), (2 * ORB_DEV) ** -0.5, 1.0, ((1, 16),), jnp.float32),
        "accumulated": noise(key_list[4], (ORBS, NZ, NY * NX), 1.0, 6.0, ((0, 16), (1, 2)), jnp.float32),
        "panel": jax.random.randint(key_list[5], (1,), 0, N_BAND * 4096).astype(jnp.int32),
    }


coefs = (-5369.0 / 1800.0, 12.0 / 7.0, -15.0 / 56.0, 10.0 / 189.0, -1.0 / 112.0, 2.0 / 1925.0, -1.0 / 16632.0)


def apply_filter(cur, prev, potential):
    lap = 3.0 * coefs[0] * cur
    for step in range(1, 7):
        for axis in (1, 2, 3):
            lap = lap + coefs[step] * (jnp.roll(cur, step, axis) + jnp.roll(cur, -step, axis))
    ham = -2.0 * lap + potential[None] * cur
    return (ham - 36.0 * cur) / 14.0 - prev


def reference(orbitals, previous, potential, rotation, accumulated, panel):
    shape = orbitals.shape
    grid = (NZ, NY, NX)
    cur = orbitals.reshape((N_BAND, ORB_DEV) + grid)
    prev = previous.reshape((N_BAND, ORB_DEV) + grid)
    field = potential.reshape(grid)
    filtered = lax.map(lambda pair: apply_filter(pair[0], pair[1], field), (cur, prev)).reshape(shape)
    which = (panel[0] % (N_BAND // 2)).astype(jnp.int32)
    start = (which * PANEL).astype(jnp.int32)
    block = lax.dynamic_slice_in_dim(filtered, start, PANEL, 0).reshape(PANEL, -1)
    rows = lax.dynamic_slice_in_dim(rotation, start, PANEL, 0)
    product = lax.dot_general(rows, block, (((0,), (0,)), ((), ())), precision=lax.Precision.HIGHEST, preferred_element_type=jnp.float32)
    rotated = accumulated + product.reshape(shape)
    return filtered, rotated
```

```python
import functools

import jax
import jax.numpy as jnp
import numpy as np
from jax import lax
from jax.experimental import pallas as pl
from jax.experimental.pallas import tpu as pltpu
from jax.sharding import PartitionSpec as P

NX = 64
REACH = 6
LANES = 128
PAD = REACH * NX
PARTS = 2
WINDOW = 6
LAG_X = 2
LAG_Z = 2
LAG_C = 2
MESH = pl.DeviceIdType.MESH

coefs = (
    -5369.0 / 1800.0,
    12.0 / 7.0,
    -15.0 / 56.0,
    10.0 / 189.0,
    -1.0 / 112.0,
    2.0 / 1925.0,
    -1.0 / 16632.0,
)
scaled = tuple(-c / 7.0 for c in coefs)


def z_tables(planes, domains):
    def weight(distance):
        distance = abs(distance)
        return scaled[distance] if 0 < distance <= REACH else 0.0

    own = np.zeros((planes, planes))
    lower = np.zeros((planes, planes))
    upper = np.zeros((planes, planes))
    for r in range(planes):
        for z in range(planes):
            j = (z - r) % planes
            own[r, z] = 3.0 * scaled[0] if j == z else weight(j - z)
            lower[r, z] = weight(j - planes - z)
            upper[r, z] = weight(j + planes - z)
    sets = [own, lower + upper] if domains == 2 else [own, lower, upper]
    table = np.stack(sets).astype(np.float32)
    return np.broadcast_to(table[..., None], table.shape + (LANES,)).copy()


def x_matrix():
    matrix = np.zeros((LANES, LANES), np.float64)
    for col in range(LANES):
        base = col // NX * NX
        for step in range(1, REACH + 1):
            for sign in (1, -1):
                matrix[base + (col - base + sign * step) % NX, col] += scaled[step]
    return matrix.astype(np.float32)


def kernel(
    domains, bands,
    sel, rows, orb, prev, pot, acc, table, xmat,
    out, rot,
    own, prv, total, fil, halo, from_x, right, left, block, other,
    in_sem, h_send, h_recv, x_send, x_recv, r_send, r_recv, l_send, l_recv,
    c_send, c_recv, o_sem, t_sem,
):
    orbs, planes, cells = orb.shape
    width = cells // PARTS
    count = orbs * PARTS
    lines = bands // 4
    sides = 1 if domains == 2 else 2

    d = lax.axis_index("domain")
    b = lax.axis_index("band")
    core = b % 2
    px = (b // 2) % 2
    pz = b // 4
    core_to = b + 1 - 2 * core
    x_to = b + 2 - 4 * px
    z_up = b + 4
    z_down = b - 4
    d_up = (d + 1) % domains
    d_down = (d + domains - 1) % domains
    d_to = (d_up,) if sides == 1 else (d_up, d_down)

    has_up = pz < lines - 1
    has_down = pz > 0

    def at(ref, i):
        return ref.at[i % orbs, :, pl.ds(pl.multiple_of(i // orbs * width, LANES), width)]

    def load(ref, i):
        return ref[i % orbs, :, pl.ds(pl.multiple_of(i // orbs * width, LANES), width)]

    def store(ref, i, value):
        ref[i % orbs, :, pl.ds(pl.multiple_of(i // orbs * width, LANES), width)] = value

    def remote(src, dst, ss, rs, to):
        return pltpu.make_async_remote_copy(
            src_ref=src, dst_ref=dst, send_sem=ss, recv_sem=rs,
            device_id={"domain": to[0], "band": to[1]}, device_id_type=MESH,
        )

    def halo_copy(s, i):
        return remote(at(orb, i), at(halo.at[s], i), h_send.at[s, i], h_recv.at[s, i], (d_to[s], b))

    def x_copy(i):
        return remote(at(fil, i), at(from_x, i), x_send.at[i], x_recv.at[i], (d, x_to))

    def right_copy(i):
        return remote(at(right, i), at(right, i), r_send.at[i], r_recv.at[i], (d, z_up))

    def left_copy(i):
        return remote(at(left, i), at(left, i), l_send.at[i], l_recv.at[i], (d, z_down))

    def core_copy(i):
        return remote(at(block, i), at(other, i), c_send.at[i], c_recv.at[i], (d, core_to))

    def out_copy(i):
        return pltpu.make_async_copy(at(fil, i), at(out, i), o_sem.at[i])

    def total_copy(p):
        part = pl.ds(p * width, width)
        return pltpu.make_async_copy(total.at[:, :, part], rot.at[:, :, part], t_sem.at[p])

    loads = [
        pltpu.make_async_copy(orb, own.at[:, :, pl.ds(PAD, cells)], in_sem.at[0]),
        pltpu.make_async_copy(
            orb.at[:, :, pl.ds(cells - PAD, PAD)], own.at[:, :, pl.ds(0, PAD)], in_sem.at[1]
        ),
        pltpu.make_async_copy(
            orb.at[:, :, pl.ds(0, PAD)], own.at[:, :, pl.ds(PAD + cells, PAD)], in_sem.at[2]
        ),
        pltpu.make_async_copy(prev, prv, in_sem.at[3]),
        pltpu.make_async_copy(acc, total, in_sem.at[4]),
    ]
    for copy in loads:
        copy.start()

    barrier = pltpu.get_barrier_semaphore()

    def greet(to):
        pl.semaphore_signal(
            barrier, inc=1, device_id={"domain": to[0], "band": to[1]}, device_id_type=MESH
        )

    for t in d_to:
        greet((t, b))
    greet((d, core_to))
    greet((d, x_to))

    @pl.when(has_up)
    def _():
        greet((d, z_up))

    @pl.when(has_down)
    def _():
        greet((d, z_down))

    peers = 2 + sides + jnp.where(has_up, 1, 0) + jnp.where(has_down, 1, 0)
    pl.semaphore_wait(barrier, peers)

    for i in range(min(WINDOW, count)):
        for s in range(sides):
            halo_copy(s, i).start()
    for copy in loads:
        copy.wait()

    shape = (planes, width)
    same_x = jnp.broadcast_to(sel[0], shape) != 0
    same_z = jnp.broadcast_to(sel[1], shape) != 0
    below = jnp.broadcast_to(sel[2], shape) != 0
    pieces = width // LANES

    def filter_chunk(i):
        o = i % orbs
        start = pl.multiple_of(i // orbs * width, LANES)
        wide = own[o, :, pl.ds(start, width + 2 * PAD)]
        half = pltpu.roll(wide, NX, 1)
        mid = wide[:, PAD : PAD + width]
        result = mid * ((pot[:, pl.ds(start, width)] - 36.0) * (1.0 / 14.0)) - load(prv, i)
        for step in range(1, REACH + 1):
            if step % 2 == 0:
                lo, hi, src = PAD - step * NX, PAD + step * NX, wide
            else:
                lo, hi, src = PAD - (step - 1) * NX, PAD + (step + 1) * NX, half
            result = result + scaled[step] * (src[:, lo : lo + width] + src[:, hi : hi + width])
        tall = jnp.concatenate(
            [mid[:, p * LANES : (p + 1) * LANES] for p in range(pieces)], axis=0
        )
        mixed = lax.dot_general(
            tall, xmat[...], (((1,), (0,)), ((), ())),
            precision=lax.Precision.HIGHEST, preferred_element_type=jnp.float32,
        )
        cols = []
        near = [load(halo.at[s], i) for s in range(sides)]
        for p in range(pieces):
            cut = slice(p * LANES, (p + 1) * LANES)
            col = result[:, cut] + mixed[p * planes : (p + 1) * planes]
            for q, src in enumerate([mid] + near):
                piece = src[:, cut]
                for r in range(planes):
                    turned = piece if r == 0 else pltpu.roll(piece, r, 0)
                    col = col + table[q, r] * turned
            cols.append(col)
        store(fil, i, jnp.concatenate(cols, axis=1))

    last_z = LAG_X + LAG_Z * (lines - 1)

    def inside(i):
        return (i >= 0) & (i < count)

    def step(t, carry):
        @pl.when(t < count)
        def _():
            for s in range(sides):
                halo_copy(s, t).wait_recv()

            @pl.when(t + WINDOW < count)
            def _():
                for s in range(sides):
                    halo_copy(s, t + WINDOW).start()

            filter_chunk(t)
            x_copy(t).start()
            out_copy(t).start()

        ix = t - LAG_X

        @pl.when(inside(ix))
        def _():
            x_copy(ix).wait_recv()
            store(from_x, ix, jnp.where(same_x, load(fil, ix), load(from_x, ix)))

        ir = t - LAG_X - LAG_Z * pz

        @pl.when(inside(ir))
        def _():
            @pl.when(has_down)
            def _():
                right_copy(ir).wait_recv()
                store(right, ir, jnp.where(same_z, load(from_x, ir), load(right, ir)))

            @pl.when(jnp.logical_not(has_down))
            def _():
                store(right, ir, load(from_x, ir))

            @pl.when(has_up)
            def _():
                right_copy(ir).start()

        il = t - LAG_X - LAG_Z * (lines - 1 - pz)

        @pl.when(inside(il))
        def _():
            @pl.when(has_up)
            def _():
                left_copy(il).wait_recv()
                store(left, il, jnp.where(same_z, load(from_x, il), load(left, il)))

            @pl.when(jnp.logical_not(has_up))
            def _():
                store(left, il, load(from_x, il))

            @pl.when(has_down)
            def _():
                left_copy(il).start()

        ib = t - last_z

        @pl.when(inside(ib))
        def _():
            store(block, ib, jnp.where(below, load(right, ib), load(left, ib)))
            core_copy(ib).start()

        ic = t - last_z - LAG_C

        @pl.when(inside(ic))
        def _():
            core_copy(ic).wait_recv()
            mine = load(block, ic)
            theirs = load(other, ic)
            o = ic % orbs
            part = pl.ds(pl.multiple_of(ic // orbs * width, LANES), width)
            for j in range(orbs):
                total[j, :, part] = total[j, :, part] + (
                    rows[core * orbs + o, j] * mine + rows[(1 - core) * orbs + o, j] * theirs
                )

        return carry

    lax.fori_loop(0, count + last_z + LAG_C, step, 0)
    for p in range(PARTS):
        total_copy(p).start()

    def drain(i, carry):
        for s in range(sides):
            halo_copy(s, i).wait_send()
        x_copy(i).wait_send()
        core_copy(i).wait_send()
        out_copy(i).wait()

        @pl.when(has_up)
        def _():
            right_copy(i).wait_send()

        @pl.when(has_down)
        def _():
            left_copy(i).wait_send()

        return carry

    lax.fori_loop(0, count, drain, 0)
    for p in range(PARTS):
        total_copy(p).wait()


def local(orbitals, previous, potential, rotation, accumulated, panel):
    domains = lax.axis_size("domain")
    bands = lax.axis_size("band")
    orbs, planes, cells = orbitals.shape
    pair = panel[0] % (bands // 2)
    rows = lax.dynamic_slice_in_dim(rotation, pair * 2 * orbs, 2 * orbs, 0)
    chip = lax.axis_index("band") // 2
    sel = jnp.stack(
        [pair % 2 == chip % 2, pair // 2 == chip // 2, pair // 2 <= chip // 2]
    ).astype(jnp.int32)
    table = jnp.asarray(z_tables(planes, domains))
    xmat = jnp.asarray(x_matrix())
    count = orbs * PARTS
    sides = 1 if domains == 2 else 2
    full = pltpu.VMEM(orbitals.shape, jnp.float32)
    dma = pltpu.SemaphoreType.DMA
    smem = pl.BlockSpec(memory_space=pltpu.SMEM)
    vmem = pl.BlockSpec(memory_space=pltpu.VMEM)
    hbm = pl.BlockSpec(memory_space=pl.ANY)
    shape = jax.ShapeDtypeStruct(orbitals.shape, jnp.float32)
    return pl.pallas_call(
        functools.partial(kernel, domains, bands),
        out_shape=(shape, shape),
        in_specs=[smem, smem, hbm, hbm, vmem, hbm, vmem, vmem],
        out_specs=(hbm, hbm),
        scratch_shapes=[
            pltpu.VMEM((orbs, planes, cells + 2 * PAD), jnp.float32),
            full,
            full,
            full,
            pltpu.VMEM((sides,) + orbitals.shape, jnp.float32),
            full, full, full, full, full,
            dma((5,)),
            dma((sides, count)), dma((sides, count)),
            dma((count,)), dma((count,)), dma((count,)), dma((count,)),
            dma((count,)), dma((count,)), dma((count,)), dma((count,)),
            dma((count,)), dma((PARTS,)),
        ],
        compiler_params=pltpu.CompilerParams(
            collective_id=0, has_side_effects=True, vmem_limit_bytes=48 * 1024 * 1024
        ),
        cost_estimate=pl.CostEstimate(
            flops=200 * orbs * planes * cells, bytes_accessed=40 * orbs * planes * cells,
            transcendentals=0,
        ),
    )(sel, rows, orbitals, previous, potential, accumulated, table, xmat)


def solution(mesh):
    in_specs = (
        P("band", "domain", None),
        P("band", "domain", None),
        P("domain", None),
        P(None, "band"),
        P("band", "domain", None),
        P(),
    )
    out_specs = (P("band", "domain", None), P("band", "domain", None))
    return jax.shard_map(local, mesh=mesh, in_specs=in_specs, out_specs=out_specs, check_vma=False)
```

```python
import functools

import jax
import jax.numpy as jnp
import numpy as np
from jax import lax
from jax.experimental import pallas as pl
from jax.experimental.pallas import tpu as pltpu
from jax.sharding import PartitionSpec as P

NX = 64
REACH = 6
LANES = 128
PAD = REACH * NX
PARTS = 2
WINDOW = 6
LAG_X = 3
LAG_Z = 3
LAG_C = 2
MESH = pl.DeviceIdType.MESH

coefs = (
    -5369.0 / 1800.0,
    12.0 / 7.0,
    -15.0 / 56.0,
    10.0 / 189.0,
    -1.0 / 112.0,
    2.0 / 1925.0,
    -1.0 / 16632.0,
)
scaled = tuple(-c / 7.0 for c in coefs)


def z_tables(planes, domains):
    def weight(distance):
        distance = abs(distance)
        return scaled[distance] if 0 < distance <= REACH else 0.0

    own = np.zeros((planes, planes))
    lower = np.zeros((planes, planes))
    upper = np.zeros((planes, planes))
    for r in range(planes):
        for z in range(planes):
            j = (z - r) % planes
            own[r, z] = 3.0 * scaled[0] if j == z else weight(j - z)
            lower[r, z] = weight(j - planes - z)
            upper[r, z] = weight(j + planes - z)
    sets = [own, lower + upper] if domains == 2 else [own, lower, upper]
    table = np.stack(sets).astype(np.float32)
    return np.broadcast_to(table[..., None], table.shape + (LANES,)).copy()


def x_matrix():
    matrix = np.zeros((LANES, LANES), np.float64)
    for col in range(LANES):
        base = col // NX * NX
        for step in range(1, REACH + 1):
            for sign in (1, -1):
                matrix[base + (col - base + sign * step) % NX, col] += scaled[step]
    return matrix.astype(np.float32)


def kernel(
    domains, bands,
    sel, rows, orb, prev, pot, acc, table, xmat,
    out, rot,
    own, prv, total, fil, halo, from_x, right, left, block, other,
    in_sem, h_send, h_recv, x_send, x_recv, r_send, r_recv, l_send, l_recv,
    c_send, c_recv, o_sem, t_sem,
):
    orbs, planes, cells = orb.shape
    width = cells // PARTS
    count = orbs * PARTS
    lines = bands // 4
    sides = 1 if domains == 2 else 2

    d = lax.axis_index("domain")
    b = lax.axis_index("band")
    core = b % 2
    px = (b // 2) % 2
    pz = b // 4
    core_to = b + 1 - 2 * core
    x_to = b + 2 - 4 * px
    z_up = b + 4
    z_down = b - 4
    d_up = (d + 1) % domains
    d_down = (d + domains - 1) % domains
    d_to = (d_up,) if sides == 1 else (d_up, d_down)

    has_up = pz < lines - 1
    has_down = pz > 0

    def at(ref, i):
        return ref.at[i % orbs, :, pl.ds(pl.multiple_of(i // orbs * width, LANES), width)]

    def load(ref, i):
        return ref[i % orbs, :, pl.ds(pl.multiple_of(i // orbs * width, LANES), width)]

    def store(ref, i, value):
        ref[i % orbs, :, pl.ds(pl.multiple_of(i // orbs * width, LANES), width)] = value

    def remote(src, dst, ss, rs, to):
        return pltpu.make_async_remote_copy(
            src_ref=src, dst_ref=dst, send_sem=ss, recv_sem=rs,
            device_id={"domain": to[0], "band": to[1]}, device_id_type=MESH,
        )

    def halo_copy(s, i):
        return remote(at(orb, i), at(halo.at[s], i), h_send.at[s, i], h_recv.at[s, i], (d_to[s], b))

    def x_copy(i):
        return remote(at(fil, i), at(from_x, i), x_send.at[i], x_recv.at[i], (d, x_to))

    def right_copy(i):
        return remote(at(right, i), at(right, i), r_send.at[i], r_recv.at[i], (d, z_up))

    def left_copy(i):
        return remote(at(left, i), at(left, i), l_send.at[i], l_recv.at[i], (d, z_down))

    def core_copy(i):
        return remote(at(block, i), at(other, i), c_send.at[i], c_recv.at[i], (d, core_to))

    def out_copy(i):
        return pltpu.make_async_copy(at(fil, i), at(out, i), o_sem.at[i])

    def total_copy(p):
        part = pl.ds(p * width, width)
        return pltpu.make_async_copy(total.at[:, :, part], rot.at[:, :, part], t_sem.at[p])

    loads = [
        pltpu.make_async_copy(orb, own.at[:, :, pl.ds(PAD, cells)], in_sem.at[0]),
        pltpu.make_async_copy(
            orb.at[:, :, pl.ds(cells - PAD, PAD)], own.at[:, :, pl.ds(0, PAD)], in_sem.at[1]
        ),
        pltpu.make_async_copy(
            orb.at[:, :, pl.ds(0, PAD)], own.at[:, :, pl.ds(PAD + cells, PAD)], in_sem.at[2]
        ),
        pltpu.make_async_copy(prev, prv, in_sem.at[3]),
        pltpu.make_async_copy(acc, total, in_sem.at[4]),
    ]
    for copy in loads:
        copy.start()

    barrier = pltpu.get_barrier_semaphore()

    def greet(to):
        pl.semaphore_signal(
            barrier, inc=1, device_id={"domain": to[0], "band": to[1]}, device_id_type=MESH
        )

    for t in d_to:
        greet((t, b))
    greet((d, core_to))
    greet((d, x_to))

    @pl.when(has_up)
    def _():
        greet((d, z_up))

    @pl.when(has_down)
    def _():
        greet((d, z_down))

    peers = 2 + sides + jnp.where(has_up, 1, 0) + jnp.where(has_down, 1, 0)
    pl.semaphore_wait(barrier, peers)

    for i in range(min(WINDOW, count)):
        for s in range(sides):
            halo_copy(s, i).start()
    for copy in loads:
        copy.wait()

    shape = (planes, width)
    same_x = jnp.broadcast_to(sel[0], shape) != 0
    same_z = jnp.broadcast_to(sel[1], shape) != 0
    below = jnp.broadcast_to(sel[2], shape) != 0
    pieces = width // LANES

    def filter_chunk(i):
        o = i % orbs
        start = pl.multiple_of(i // orbs * width, LANES)
        wide = own[o, :, pl.ds(start, width + 2 * PAD)]
        half = pltpu.roll(wide, NX, 1)
        mid = wide[:, PAD : PAD + width]
        result = mid * ((pot[:, pl.ds(start, width)] - 36.0) * (1.0 / 14.0)) - load(prv, i)
        for step in range(1, REACH + 1):
            if step % 2 == 0:
                lo, hi, src = PAD - step * NX, PAD + step * NX, wide
            else:
                lo, hi, src = PAD - (step - 1) * NX, PAD + (step + 1) * NX, half
            result = result + scaled[step] * (src[:, lo : lo + width] + src[:, hi : hi + width])
        tall = jnp.concatenate(
            [mid[:, p * LANES : (p + 1) * LANES] for p in range(pieces)], axis=0
        )
        mixed = lax.dot_general(
            tall, xmat[...], (((1,), (0,)), ((), ())),
            precision=lax.Precision.HIGHEST, preferred_element_type=jnp.float32,
        )
        cols = []
        near = [load(halo.at[s], i) for s in range(sides)]
        for p in range(pieces):
            cut = slice(p * LANES, (p + 1) * LANES)
            col = result[:, cut] + mixed[p * planes : (p + 1) * planes]
            for q, src in enumerate([mid] + near):
                piece = src[:, cut]
                for r in range(planes):
                    turned = piece if r == 0 else pltpu.roll(piece, r, 0)
                    col = col + table[q, r] * turned
            cols.append(col)
        store(fil, i, jnp.concatenate(cols, axis=1))

    last_z = LAG_X + LAG_Z * (lines - 1)

    def inside(i):
        return (i >= 0) & (i < count)

    def step(t, carry):
        @pl.when(t < count)
        def _():
            for s in range(sides):
                halo_copy(s, t).wait_recv()

            @pl.when(t + WINDOW < count)
            def _():
                for s in range(sides):
                    halo_copy(s, t + WINDOW).start()

            filter_chunk(t)
            x_copy(t).start()
            out_copy(t).start()

        ix = t - LAG_X

        @pl.when(inside(ix))
        def _():
            x_copy(ix).wait_recv()
            store(from_x, ix, jnp.where(same_x, load(fil, ix), load(from_x, ix)))

        ir = t - LAG_X - LAG_Z * pz

        @pl.when(inside(ir))
        def _():
            @pl.when(has_down)
            def _():
                right_copy(ir).wait_recv()
                store(right, ir, jnp.where(same_z, load(from_x, ir), load(right, ir)))

            @pl.when(jnp.logical_not(has_down))
            def _():
                store(right, ir, load(from_x, ir))

            @pl.when(has_up)
            def _():
                right_copy(ir).start()

        il = t - LAG_X - LAG_Z * (lines - 1 - pz)

        @pl.when(inside(il))
        def _():
            @pl.when(has_up)
            def _():
                left_copy(il).wait_recv()
                store(left, il, jnp.where(same_z, load(from_x, il), load(left, il)))

            @pl.when(jnp.logical_not(has_up))
            def _():
                store(left, il, load(from_x, il))

            @pl.when(has_down)
            def _():
                left_copy(il).start()

        ib = t - last_z

        @pl.when(inside(ib))
        def _():
            store(block, ib, jnp.where(below, load(right, ib), load(left, ib)))
            core_copy(ib).start()

        ic = t - last_z - LAG_C

        @pl.when(inside(ic))
        def _():
            core_copy(ic).wait_recv()
            mine = load(block, ic)
            theirs = load(other, ic)
            o = ic % orbs
            part = pl.ds(pl.multiple_of(ic // orbs * width, LANES), width)
            for j in range(orbs):
                total[j, :, part] = total[j, :, part] + (
                    rows[core * orbs + o, j] * mine + rows[(1 - core) * orbs + o, j] * theirs
                )

        return carry

    lax.fori_loop(0, count + last_z + LAG_C, step, 0)
    for p in range(PARTS):
        total_copy(p).start()

    def drain(i, carry):
        for s in range(sides):
            halo_copy(s, i).wait_send()
        x_copy(i).wait_send()
        core_copy(i).wait_send()
        out_copy(i).wait()

        @pl.when(has_up)
        def _():
            right_copy(i).wait_send()

        @pl.when(has_down)
        def _():
            left_copy(i).wait_send()

        return carry

    lax.fori_loop(0, count, drain, 0)
    for p in range(PARTS):
        total_copy(p).wait()


def local(orbitals, previous, potential, rotation, accumulated, panel):
    domains = lax.axis_size("domain")
    bands = lax.axis_size("band")
    orbs, planes, cells = orbitals.shape
    pair = panel[0] % (bands // 2)
    rows = lax.dynamic_slice_in_dim(rotation, pair * 2 * orbs, 2 * orbs, 0)
    chip = lax.axis_index("band") // 2
    sel = jnp.stack(
        [pair % 2 == chip % 2, pair // 2 == chip // 2, pair // 2 <= chip // 2]
    ).astype(jnp.int32)
    table = jnp.asarray(z_tables(planes, domains))
    xmat = jnp.asarray(x_matrix())
    count = orbs * PARTS
    sides = 1 if domains == 2 else 2
    full = pltpu.VMEM(orbitals.shape, jnp.float32)
    dma = pltpu.SemaphoreType.DMA
    smem = pl.BlockSpec(memory_space=pltpu.SMEM)
    vmem = pl.BlockSpec(memory_space=pltpu.VMEM)
    hbm = pl.BlockSpec(memory_space=pl.ANY)
    shape = jax.ShapeDtypeStruct(orbitals.shape, jnp.float32)
    return pl.pallas_call(
        functools.partial(kernel, domains, bands),
        out_shape=(shape, shape),
        in_specs=[smem, smem, hbm, hbm, vmem, hbm, vmem, vmem],
        out_specs=(hbm, hbm),
        scratch_shapes=[
            pltpu.VMEM((orbs, planes, cells + 2 * PAD), jnp.float32),
            full,
            full,
            full,
            pltpu.VMEM((sides,) + orbitals.shape, jnp.float32),
            full, full, full, full, full,
            dma((5,)),
            dma((sides, count)), dma((sides, count)),
            dma((count,)), dma((count,)), dma((count,)), dma((count,)),
            dma((count,)), dma((count,)), dma((count,)), dma((count,)),
            dma((count,)), dma((PARTS,)),
        ],
        compiler_params=pltpu.CompilerParams(
            collective_id=0, has_side_effects=True, vmem_limit_bytes=48 * 1024 * 1024
        ),
        cost_estimate=pl.CostEstimate(
            flops=200 * orbs * planes * cells, bytes_accessed=40 * orbs * planes * cells,
            transcendentals=0,
        ),
    )(sel, rows, orbitals, previous, potential, accumulated, table, xmat)


def solution(mesh):
    in_specs = (
        P("band", "domain", None),
        P("band", "domain", None),
        P("domain", None),
        P(None, "band"),
        P("band", "domain", None),
        P(),
    )
    out_specs = (P("band", "domain", None), P("band", "domain", None))
    return jax.shard_map(local, mesh=mesh, in_specs=in_specs, out_specs=out_specs, check_vma=False)
```

```python
import functools

import jax
import jax.numpy as jnp
import numpy as np
from jax import lax
from jax.experimental import pallas as pl
from jax.experimental.pallas import tpu as pltpu
from jax.sharding import PartitionSpec as P

NX = 64
REACH = 6
LANES = 128
PAD = REACH * NX
PARTS = 2
WINDOW = 6
LAG_X = 3
LAG_Z = 3
LAG_C = 2
MESH = pl.DeviceIdType.MESH

coefs = (
    -5369.0 / 1800.0,
    12.0 / 7.0,
    -15.0 / 56.0,
    10.0 / 189.0,
    -1.0 / 112.0,
    2.0 / 1925.0,
    -1.0 / 16632.0,
)
scaled = tuple(-c / 7.0 for c in coefs)


def z_tables(planes, domains):
    def weight(distance):
        distance = abs(distance)
        return scaled[distance] if 0 < distance <= REACH else 0.0

    own = np.zeros((planes, planes))
    lower = np.zeros((planes, planes))
    upper = np.zeros((planes, planes))
    for r in range(planes):
        for z in range(planes):
            j = (z - r) % planes
            own[r, z] = 3.0 * scaled[0] if j == z else weight(j - z)
            lower[r, z] = weight(j - planes - z)
            upper[r, z] = weight(j + planes - z)
    sets = [own, lower + upper] if domains == 2 else [own, lower, upper]
    table = np.stack(sets).astype(np.float32)
    return np.broadcast_to(table[..., None], table.shape + (LANES,)).copy()


def x_matrix():
    matrix = np.zeros((LANES, LANES), np.float64)
    for col in range(LANES):
        base = col // NX * NX
        for step in range(1, REACH + 1):
            for sign in (1, -1):
                matrix[base + (col - base + sign * step) % NX, col] += scaled[step]
    return matrix.astype(np.float32)


def kernel(
    domains, bands,
    sel, rows, orb, prev, pot, acc, table, xmat,
    out, rot,
    own, prv, total, fil, halo, from_x, right, left, block, other,
    in_sem, h_send, h_recv, x_send, x_recv, r_send, r_recv, l_send, l_recv,
    c_send, c_recv, o_sem, t_sem,
):
    orbs, planes, cells = orb.shape
    width = cells // PARTS
    count = orbs * PARTS
    lines = bands // 4
    sides = 1 if domains == 2 else 2

    d = lax.axis_index("domain")
    b = lax.axis_index("band")
    core = b % 2
    px = (b // 2) % 2
    pz = b // 4
    core_to = b + 1 - 2 * core
    x_to = b + 2 - 4 * px
    z_up = b + 4
    z_down = b - 4
    d_up = (d + 1) % domains
    d_down = (d + domains - 1) % domains
    d_to = (d_up,) if sides == 1 else (d_up, d_down)

    has_up = pz < lines - 1
    has_down = pz > 0

    def at(ref, i):
        return ref.at[i % orbs, :, pl.ds(pl.multiple_of(i // orbs * width, LANES), width)]

    def load(ref, i):
        return ref[i % orbs, :, pl.ds(pl.multiple_of(i // orbs * width, LANES), width)]

    def store(ref, i, value):
        ref[i % orbs, :, pl.ds(pl.multiple_of(i // orbs * width, LANES), width)] = value

    def remote(src, dst, ss, rs, to):
        return pltpu.make_async_remote_copy(
            src_ref=src, dst_ref=dst, send_sem=ss, recv_sem=rs,
            device_id={"domain": to[0], "band": to[1]}, device_id_type=MESH,
        )

    def halo_copy(s, i):
        return remote(at(orb, i), at(halo.at[s], i), h_send.at[s, i], h_recv.at[s, i], (d_to[s], b))

    def x_copy(i):
        return remote(at(fil, i), at(from_x, i), x_send.at[i], x_recv.at[i], (d, x_to))

    def right_copy(i):
        return remote(at(right, i), at(right, i), r_send.at[i], r_recv.at[i], (d, z_up))

    def left_copy(i):
        return remote(at(left, i), at(left, i), l_send.at[i], l_recv.at[i], (d, z_down))

    def core_copy(i):
        return remote(at(block, i), at(other, i), c_send.at[i], c_recv.at[i], (d, core_to))

    def out_copy(i):
        return pltpu.make_async_copy(at(fil, i), at(out, i), o_sem.at[i])

    def total_copy(p):
        part = pl.ds(p * width, width)
        return pltpu.make_async_copy(total.at[:, :, part], rot.at[:, :, part], t_sem.at[p])

    loads = [
        pltpu.make_async_copy(orb, own.at[:, :, pl.ds(PAD, cells)], in_sem.at[0]),
        pltpu.make_async_copy(
            orb.at[:, :, pl.ds(cells - PAD, PAD)], own.at[:, :, pl.ds(0, PAD)], in_sem.at[1]
        ),
        pltpu.make_async_copy(
            orb.at[:, :, pl.ds(0, PAD)], own.at[:, :, pl.ds(PAD + cells, PAD)], in_sem.at[2]
        ),
        pltpu.make_async_copy(prev, prv, in_sem.at[3]),
        pltpu.make_async_copy(acc, total, in_sem.at[4]),
    ]
    for copy in loads:
        copy.start()

    barrier = pltpu.get_barrier_semaphore()

    def greet(to):
        pl.semaphore_signal(
            barrier, inc=1, device_id={"domain": to[0], "band": to[1]}, device_id_type=MESH
        )

    for t in d_to:
        greet((t, b))
    greet((d, core_to))
    greet((d, x_to))

    @pl.when(has_up)
    def _():
        greet((d, z_up))

    @pl.when(has_down)
    def _():
        greet((d, z_down))

    peers = 2 + sides + jnp.where(has_up, 1, 0) + jnp.where(has_down, 1, 0)
    pl.semaphore_wait(barrier, peers)

    for i in range(min(WINDOW, count)):
        for s in range(sides):
            halo_copy(s, i).start()
    for copy in loads[:4]:
        copy.wait()

    shape = (planes, width)
    same_x = jnp.broadcast_to(sel[0], shape) != 0
    same_z = jnp.broadcast_to(sel[1], shape) != 0
    below = jnp.broadcast_to(sel[2], shape) != 0
    pieces = width // LANES

    def filter_chunk(i):
        o = i % orbs
        start = pl.multiple_of(i // orbs * width, LANES)
        wide = own[o, :, pl.ds(start, width + 2 * PAD)]
        half = pltpu.roll(wide, NX, 1)
        mid = wide[:, PAD : PAD + width]
        result = mid * ((pot[:, pl.ds(start, width)] - 36.0) * (1.0 / 14.0)) - load(prv, i)
        for step in range(1, REACH + 1):
            if step % 2 == 0:
                lo, hi, src = PAD - step * NX, PAD + step * NX, wide
            else:
                lo, hi, src = PAD - (step - 1) * NX, PAD + (step + 1) * NX, half
            result = result + scaled[step] * (src[:, lo : lo + width] + src[:, hi : hi + width])
        tall = jnp.concatenate(
            [mid[:, p * LANES : (p + 1) * LANES] for p in range(pieces)], axis=0
        )
        mixed = lax.dot_general(
            tall, xmat[...], (((1,), (0,)), ((), ())),
            precision=lax.Precision.HIGHEST, preferred_element_type=jnp.float32,
        )
        cols = []
        near = [load(halo.at[s], i) for s in range(sides)]
        for p in range(pieces):
            cut = slice(p * LANES, (p + 1) * LANES)
            col = result[:, cut] + mixed[p * planes : (p + 1) * planes]
            for q, src in enumerate([mid] + near):
                piece = src[:, cut]
                for r in range(planes):
                    turned = piece if r == 0 else pltpu.roll(piece, r, 0)
                    col = col + table[q, r] * turned
            cols.append(col)
        store(fil, i, jnp.concatenate(cols, axis=1))

    last_z = LAG_X + LAG_Z * (lines - 1)

    def inside(i):
        return (i >= 0) & (i < count)

    def step(t, carry):
        @pl.when(t == 1)
        def _():
            loads[4].wait()

        ix = t - LAG_X

        @pl.when(inside(ix))
        def _():
            x_copy(ix).wait_recv()
            store(from_x, ix, jnp.where(same_x, load(fil, ix), load(from_x, ix)))

        ir = t - LAG_X - LAG_Z * pz

        @pl.when(inside(ir))
        def _():
            @pl.when(has_down)
            def _():
                right_copy(ir).wait_recv()
                store(right, ir, jnp.where(same_z, load(from_x, ir), load(right, ir)))

            @pl.when(jnp.logical_not(has_down))
            def _():
                store(right, ir, load(from_x, ir))

            @pl.when(has_up)
            def _():
                right_copy(ir).start()

        il = t - LAG_X - LAG_Z * (lines - 1 - pz)

        @pl.when(inside(il))
        def _():
            @pl.when(has_up)
            def _():
                left_copy(il).wait_recv()
                store(left, il, jnp.where(same_z, load(from_x, il), load(left, il)))

            @pl.when(jnp.logical_not(has_up))
            def _():
                store(left, il, load(from_x, il))

            @pl.when(has_down)
            def _():
                left_copy(il).start()

        ib = t - last_z

        @pl.when(inside(ib))
        def _():
            store(block, ib, jnp.where(below, load(right, ib), load(left, ib)))
            core_copy(ib).start()

        @pl.when(t < count)
        def _():
            for s in range(sides):
                halo_copy(s, t).wait_recv()

            @pl.when(t + WINDOW < count)
            def _():
                for s in range(sides):
                    halo_copy(s, t + WINDOW).start()

            filter_chunk(t)
            x_copy(t).start()
            out_copy(t).start()

        ic = t - last_z - LAG_C

        @pl.when(inside(ic))
        def _():
            core_copy(ic).wait_recv()
            mine = load(block, ic)
            theirs = load(other, ic)
            o = ic % orbs
            part = pl.ds(pl.multiple_of(ic // orbs * width, LANES), width)
            for j in range(orbs):
                total[j, :, part] = total[j, :, part] + (
                    rows[core * orbs + o, j] * mine + rows[(1 - core) * orbs + o, j] * theirs
                )

        return carry

    lax.fori_loop(0, count + last_z + LAG_C, step, 0)
    for p in range(PARTS):
        total_copy(p).start()

    def drain(i, carry):
        for s in range(sides):
            halo_copy(s, i).wait_send()
        x_copy(i).wait_send()
        core_copy(i).wait_send()
        out_copy(i).wait()

        @pl.when(has_up)
        def _():
            right_copy(i).wait_send()

        @pl.when(has_down)
        def _():
            left_copy(i).wait_send()

        return carry

    lax.fori_loop(0, count, drain, 0)
    for p in range(PARTS):
        total_copy(p).wait()


def local(orbitals, previous, potential, rotation, accumulated, panel):
    domains = lax.axis_size("domain")
    bands = lax.axis_size("band")
    orbs, planes, cells = orbitals.shape
    pair = panel[0] % (bands // 2)
    rows = lax.dynamic_slice_in_dim(rotation, pair * 2 * orbs, 2 * orbs, 0)
    chip = lax.axis_index("band") // 2
    sel = jnp.stack(
        [pair % 2 == chip % 2, pair // 2 == chip // 2, pair // 2 <= chip // 2]
    ).astype(jnp.int32)
    table = jnp.asarray(z_tables(planes, domains))
    xmat = jnp.asarray(x_matrix())
    count = orbs * PARTS
    sides = 1 if domains == 2 else 2
    full = pltpu.VMEM(orbitals.shape, jnp.float32)
    dma = pltpu.SemaphoreType.DMA
    smem = pl.BlockSpec(memory_space=pltpu.SMEM)
    vmem = pl.BlockSpec(memory_space=pltpu.VMEM)
    hbm = pl.BlockSpec(memory_space=pl.ANY)
    shape = jax.ShapeDtypeStruct(orbitals.shape, jnp.float32)
    return pl.pallas_call(
        functools.partial(kernel, domains, bands),
        out_shape=(shape, shape),
        in_specs=[smem, smem, hbm, hbm, vmem, hbm, vmem, vmem],
        out_specs=(hbm, hbm),
        scratch_shapes=[
            pltpu.VMEM((orbs, planes, cells + 2 * PAD), jnp.float32),
            full,
            full,
            full,
            pltpu.VMEM((sides,) + orbitals.shape, jnp.float32),
            full, full, full, full, full,
            dma((5,)),
            dma((sides, count)), dma((sides, count)),
            dma((count,)), dma((count,)), dma((count,)), dma((count,)),
            dma((count,)), dma((count,)), dma((count,)), dma((count,)),
            dma((count,)), dma((PARTS,)),
        ],
        compiler_params=pltpu.CompilerParams(
            collective_id=0, has_side_effects=True, vmem_limit_bytes=48 * 1024 * 1024
        ),
        cost_estimate=pl.CostEstimate(
            flops=200 * orbs * planes * cells, bytes_accessed=40 * orbs * planes * cells,
            transcendentals=0,
        ),
    )(sel, rows, orbitals, previous, potential, accumulated, table, xmat)


def solution(mesh):
    in_specs = (
        P("band", "domain", None),
        P("band", "domain", None),
        P("domain", None),
        P(None, "band"),
        P("band", "domain", None),
        P(),
    )
    out_specs = (P("band", "domain", None), P("band", "domain", None))
    return jax.shard_map(local, mesh=mesh, in_specs=in_specs, out_specs=out_specs, check_vma=False)
```
